32 devices in a mesh: ops: 4 (over z), sec: 8 (over y, x, core).
Axes of the slice: x: 2, y: 2, z: 4, core: 2. Of those that a mesh axis runs over, the one named last changes fastest.
Arguments:
- wave_vectors: float32 [2, 8, 8, 128, 128], P(None, 'sec'), may hold values from -6 to 6
- left_blocks: float32 [16, 8, 128, 128], P('ops'), may hold values from -0.1875 to 0.1875
- right_blocks: float32 [16, 8, 128, 128], P('ops', 'sec'), may hold values from -0.5 to 0.5
- left_links: int32 [16, 8], P('ops'), may hold values from 0 to 7
- right_links: int32 [16, 8], P('ops', 'sec'), may hold values from 0 to 7, as said below
Outputs:
- sigma: float32 [2, 8, 8, 128, 128], P(None, 'ops', 'sec')
The draws below stay inside these ranges and needn't reach their ends.
Inputs may be any that keep to these rules, and one draw needn't show every extreme that they name: `right_links`: each entry differs from its column index j by at most one.
All inputs are finite; a program needn't handle non-finite values.
Results may differ from the reference program's by a relative error of at most 0.0001.
Values sent between devices are 32-bit elements; how exact they have to be, the bound alone decides.
A program may use at most 128 MiB of HBM per device.

```python
import jax
import jax.numpy as jnp
from jax import lax

B = 128
V = 2
NQ = 8
PAIRS = 16


def draw_right_links(key, part):
    key = jax.random.fold_in(key, 7)
    stepping = jax.random.randint(key, (PAIRS, NQ), -1, 2)
    columns = jnp.arange(NQ, dtype=jnp.int32)[None, :]
    return jnp.clip(columns + stepping, 0, NQ - 1).astype(jnp.int32)


def with_ends(entries, key, low, high):
    longest = entries.shape.index(max(entries.shape))
    spots = []
    for shift in (0, 1):
        where = [jax.random.randint(jax.random.fold_in(key, axis), (), 0, length) for axis, length in enumerate(entries.shape)]
        where[longest] = (where[longest] + shift) % entries.shape[longest]
        spots.append(tuple(where))
    return entries.at[spots[0]].set(low).at[spots[1]].set(high)


def raised(result, key, source, target, blocks, factor):
    owner, partner = [(jnp.arange(result.shape[axis_at]) // (result.shape[axis_at] // blocks)).reshape([-1 if axis == axis_at else 1 for axis in range(result.ndim)]) for axis_at in (source, target)]
    chosen = jax.random.permutation(key, blocks)[partner]
    strong = (owner == chosen) | (owner == (partner + blocks // 2) % blocks)
    return jnp.where(strong, factor * result, result)


def levels(stream_key, dims, shards, smallest, high):
    factor_of, own = 1.0, jax.random.fold_in(stream_key, 6)
    for axis_at, parts in shards:
        heights = jnp.exp(jax.random.uniform(jax.random.fold_in(own, axis_at), (parts,), jnp.float32, smallest / len(shards), high / len(shards)))
        factor_of = factor_of * jnp.repeat(heights, dims[axis_at] // parts).reshape([-1 if axis == axis_at else 1 for axis in range(len(dims))])
    return factor_of


def centred(stream_key, shape, width, most, cuts=(), kind=jnp.bfloat16):
    array = width * jax.random.normal(stream_key, shape, jnp.float32)
    if cuts:
        array = array * levels(stream_key, shape, cuts, -0.22, 0.18)
    return jnp.clip(array, -most, most).astype(kind)


def bell_draw_with(stream_key, extent, scale, limit, shards, heavy, kind=jnp.bfloat16):
    entries = scale * jax.random.normal(stream_key, extent, jnp.float32)
    if shards:
        entries = entries * levels(stream_key, extent, shards, -0.22, 0.18)
    return jnp.clip(raised(entries, jax.random.fold_in(stream_key, 3), *heavy), -limit, limit).astype(kind)


def setup_inputs(seed: int = 0) -> dict:
    key_of = jax.random.split(jax.random.key(seed), 6)
    return {
        "wave_vectors": centred(key_of[0], (V, NQ, NQ, B, B), 1.0, 6.0, ((1, 8),), jnp.float32),
        "left_blocks": bell_draw_with(key_of[1], (PAIRS, NQ, B, B), (B * PAIRS) ** -0.5, 0.1875, ((0, 4),), (0, 1, 4, 2.0), jnp.float32),
        "right_blocks": centred(key_of[2], (PAIRS, NQ, B, B), B ** -0.5, 0.5, ((0, 4), (1, 8)), jnp.float32),
        "left_links": with_ends(jax.random.randint(key_of[3], (PAIRS, NQ), 0, NQ), jax.random.fold_in(key_of[3], 1), 0, NQ - 1).astype(jnp.int32),
        "right_links": draw_right_links(jax.random.fold_in(key_of[5], 71), 0),
    }


highest = lax.Precision.HIGHEST


def reference(wave_vectors, left_blocks, right_blocks, left_links, right_links):
    def one_pair(summed, index):
        source = jnp.take(wave_vectors, right_links[index], axis=2)
        inner = jnp.einsum('vijab,jcb->vijac', source, right_blocks[index], precision=highest)
        picked = jnp.take(inner, left_links[index], axis=1)
        added = jnp.einsum('iab,vijbc->vijac', left_blocks[index], picked, precision=highest)
        return summed + added, None

    start = jnp.zeros(wave_vectors.shape, jnp.float32)
    sigma, unused = lax.scan(one_pair, start, jnp.arange(PAIRS, dtype=jnp.int32))
    return sigma
```

```python
import functools

import jax
import jax.numpy as jnp
from jax import lax
from jax.experimental import pallas as pl
from jax.experimental.pallas import tpu as pltpu
from jax.sharding import PartitionSpec as P

f32, bf16 = jnp.float32, jnp.bfloat16
SPAN = 3


def split(x):
    hi = x.astype(bf16)
    return hi, (x - hi.astype(f32)).astype(bf16)


def dot(a, b):
    return lax.dot_general(a, b, (((1,), (0,)), ((), ())), preferred_element_type=f32)


def kernel(ns, no, psi, left, right, llinks, rlinks, out,
           wave, lv, rv, wr, inner, part, got,
           load_sem, own_sem, xs_sem, xr_sem, ss_sem, sr_sem):
    vecs, _, nq, b, _ = psi.shape
    pairs = left.shape[0]
    rows = nq // no
    o, s = lax.axis_index("ops"), lax.axis_index("sec")

    def first(t):
        return jnp.clip(t - 1, 0, nq - SPAN)

    def peer(k):
        return lax.rem(s + k, ns)

    def layer(k):
        return lax.rem(o + k, no)

    loads = [pltpu.make_async_copy(right, rv, load_sem.at[0]),
             pltpu.make_async_copy(left, lv, load_sem.at[1])]
    for c in loads:
        c.start()
    owns = [pltpu.make_async_copy(psi.at[v, 0, pl.ds(first(s), SPAN)], wave.at[v, s], own_sem.at[v])
            for v in range(vecs)]
    for c in owns:
        c.start()

    barrier = pltpu.get_barrier_semaphore()

    @pl.loop(1, ns)
    def _(k):
        pl.semaphore_signal(barrier, inc=1, device_id=(o, peer(k)), device_id_type=pl.DeviceIdType.MESH)

    @pl.loop(1, no)
    def _(k):
        pl.semaphore_signal(barrier, inc=1, device_id=(layer(k), s), device_id_type=pl.DeviceIdType.MESH)

    pl.semaphore_wait(barrier, ns - 1 + no - 1)

    def exchange(v, k):
        t = peer(k)
        return pltpu.make_async_remote_copy(
            src_ref=psi.at[v, 0, pl.ds(first(t), SPAN)], dst_ref=wave.at[v, s],
            send_sem=xs_sem.at[v, k], recv_sem=xr_sem.at[v, k],
            device_id=(o, t), device_id_type=pl.DeviceIdType.MESH)

    for v in range(vecs):
        @pl.loop(1, ns)
        def _(k):
            exchange(v, k).start()

    loads[0].wait()
    for p in range(pairs):
        hi, lo = split(rv[p, 0].T)
        wr[p, :b, :b] = hi
        wr[p, :b, b:] = lo
        wr[p, b:, :b] = hi
        wr[p, b:, b:] = jnp.zeros((b, b), bf16)

    def contract_right(v, q):
        for p in range(pairs):
            d = rlinks[p, 0] - first(s)
            x = jnp.where(d == 0, wave[v, q, 0], jnp.where(d == 1, wave[v, q, 1], wave[v, q, 2]))
            hi, lo = split(x)
            y = dot(jnp.concatenate([hi, lo], axis=1), wr[p])
            hi, lo = split(y[:, :b] + y[:, b:])
            inner[v, p, q, :, :b] = hi
            inner[v, p, q, :, b:] = lo

    def contract_left(v, i):
        pieces = [split(lv[p, i]) for p in range(pairs)]
        picked = jnp.concatenate([inner[v, p, llinks[p, i]] for p in range(pairs)], axis=0)
        y = dot(jnp.concatenate([c[0] for c in pieces], axis=1), picked)
        z = dot(jnp.concatenate([c[1] for c in pieces], axis=1), picked[:, :b])
        return y[:, :b] + y[:, b:] + z

    def scatter(v, k):
        return pltpu.make_async_remote_copy(
            src_ref=part.at[v, k], dst_ref=got.at[v, k],
            send_sem=ss_sem.at[v, k], recv_sem=sr_sem.at[v, k],
            device_id=(layer(k), s), device_id_type=pl.DeviceIdType.MESH)

    for v in range(vecs):
        owns[v].wait()
        contract_right(v, s)

        @pl.loop(1, ns)
        def _(k):
            q = lax.rem(s + ns - k, ns)
            pltpu.make_async_remote_copy(
                src_ref=psi.at[v, 0, pl.ds(0, SPAN)], dst_ref=wave.at[v, q],
                send_sem=xs_sem.at[v, k], recv_sem=xr_sem.at[v, k],
                device_id=(o, q), device_id_type=pl.DeviceIdType.MESH).wait_recv()
            contract_right(v, q)

        if v == 0:
            loads[1].wait()

        @pl.loop(1, no)
        def _(k):
            for r in range(rows):
                part[v, k, r] = contract_left(v, layer(k) * rows + r)
            scatter(v, k).start()

        for r in range(rows):
            part[v, 0, r] = contract_left(v, o * rows + r)

    for v in range(vecs):
        @pl.loop(1, no)
        def _(k):
            scatter(v, k).wait_recv()
        for r in range(rows):
            total = part[v, 0, r]
            for k in range(1, no):
                total = total + got[v, k, r]
            out[v, r, 0] = total

    for v in range(vecs):
        @pl.loop(1, ns)
        def _(k):
            exchange(v, k).wait_send()

        @pl.loop(1, no)
        def _(k):
            scatter(v, k).wait_send()


def on_device(psi, left, right, llinks, rlinks):
    ns, no = lax.axis_size("sec"), lax.axis_size("ops")
    vecs, _, nq, b, _ = psi.shape
    pairs, rows = left.shape[0], nq // no
    shapes = [((vecs, nq, SPAN, b, b), f32), (left.shape, f32), (right.shape, f32),
              ((pairs, 2 * b, 2 * b), bf16), ((vecs, pairs, nq, b, 2 * b), bf16),
              ((vecs, no, rows, b, b), f32), ((vecs, no, rows, b, b), f32)]
    need = sum(jnp.dtype(t).itemsize * functools.reduce(lambda x, y: x * y, d) for d, t in shapes)
    any_, smem, vmem = (pl.BlockSpec(memory_space=m) for m in (pl.ANY, pltpu.SMEM, pltpu.VMEM))
    return pl.pallas_call(
        functools.partial(kernel, ns, no),
        out_shape=jax.ShapeDtypeStruct((vecs, rows, 1, b, b), f32),
        in_specs=[any_, any_, any_, smem, smem],
        out_specs=vmem,
        scratch_shapes=[pltpu.VMEM(d, t) for d, t in shapes] + [
            pltpu.SemaphoreType.DMA((2,)), pltpu.SemaphoreType.DMA((vecs,)),
            pltpu.SemaphoreType.DMA((vecs, ns)), pltpu.SemaphoreType.DMA((vecs, ns)),
            pltpu.SemaphoreType.DMA((vecs, no)), pltpu.SemaphoreType.DMA((vecs, no))],
        compiler_params=pltpu.CompilerParams(
            collective_id=0, has_side_effects=True, vmem_limit_bytes=need + (6 << 20)),
    )(psi, left, right, llinks, rlinks)


def solution(mesh):
    return jax.shard_map(
        on_device,
        mesh=mesh,
        in_specs=(
            P(None, "sec", None, None, None),
            P("ops", None, None, None),
            P("ops", "sec", None, None),
            P("ops", None),
            P("ops", "sec"),
        ),
        out_specs=P(None, "ops", "sec", None, None),
        check_vma=False,
    )
```

```python
import functools

import jax
import jax.numpy as jnp
from jax import lax
from jax.experimental import pallas as pl
from jax.experimental.pallas import tpu as pltpu
from jax.sharding import PartitionSpec as P

f32, bf16 = jnp.float32, jnp.bfloat16
SPAN = 3


def split(x):
    hi = x.astype(bf16)
    return hi, (x - hi.astype(f32)).astype(bf16)


def dot(a, b):
    return lax.dot_general(a, b, (((1,), (0,)), ((), ())), preferred_element_type=f32)


def kernel(ns, no, psi, left, right, llinks, rlinks, out,
           wave, lv, rv, wr, inner, part, got,
           load_sem, own_sem, xs_sem, xr_sem, ss_sem, sr_sem):
    vecs, _, nq, b, _ = psi.shape
    pairs = left.shape[0]
    rows = nq // no
    o, s = lax.axis_index("ops"), lax.axis_index("sec")

    odd = lax.rem(s, 2)
    mate = s + 1 - 2 * odd

    def peer(k):
        return lax.rem(s + k, ns)

    def layer(k):
        return lax.rem(o + k, no)

    loads = [pltpu.make_async_copy(right, rv, load_sem.at[0]),
             pltpu.make_async_copy(left, lv, load_sem.at[1])]
    for c in loads:
        c.start()
    def window(t, go):
        for case, lo, hi in ((t == 0, 1, 3), (t == nq - 1, 0, 2), ((t > 0) & (t < nq - 1), 0, 3)):
            @pl.when(case)
            def _():
                go(pl.ds(t - 1 + lo, hi - lo), pl.ds(lo, hi - lo))

    def own(v, go):
        window(s, lambda src, dst: go(pltpu.make_async_copy(
            psi.at[v, 0, src], wave.at[v, s, dst], own_sem.at[v])))

    for v in range(vecs):
        own(v, lambda c: c.start())

    barrier = pltpu.get_barrier_semaphore()

    @pl.loop(1, ns)
    def _(k):
        pl.semaphore_signal(barrier, inc=1, device_id=(o, peer(k)), device_id_type=pl.DeviceIdType.MESH)

    @pl.loop(1, no)
    def _(k):
        pl.semaphore_signal(barrier, inc=1, device_id=(layer(k), s), device_id_type=pl.DeviceIdType.MESH)

    pl.semaphore_wait(barrier, ns - 1 + no - 1)

    def remote(src, dst, send, recv, to):
        return pltpu.make_async_remote_copy(
            src_ref=src, dst_ref=dst, send_sem=send, recv_sem=recv,
            device_id=to, device_id_type=pl.DeviceIdType.MESH)

    def partner(k, way):
        chip = lax.rem(s // 2 + ns // 2 + way * (k // 2), ns // 2)
        return 2 * chip + lax.rem(s + k, 2)

    def middle(v, row, t, k):
        return remote(psi.at[v, 0, t], wave.at[v, row, 1], xs_sem.at[v, k, 0], xr_sem.at[v, k, 0], (o, t))

    def outer(v, row, t, k, go):
        even = lax.rem(t, 2) == 0
        @pl.when(even & (t > 0))
        def _():
            go(remote(psi.at[v, 0, t - 1], wave.at[v, row, 0], xs_sem.at[v, k, 1], xr_sem.at[v, k, 1], (o, t)))
        @pl.when(jnp.logical_not(even) & (t < nq - 1))
        def _():
            go(remote(psi.at[v, 0, t + 1], wave.at[v, row, 2], xs_sem.at[v, k, 1], xr_sem.at[v, k, 1], (o, t)))

    def mated(v, t, row, go):
        window(t, lambda src, dst: go(remote(
            psi.at[v, 0, src], wave.at[v, row, dst], xs_sem.at[v, 1, 0], xr_sem.at[v, 1, 0], (o, mate))))

    def forward(v, row, slot):
        return remote(wave.at[v, row, 1], wave.at[v, row, slot], xs_sem.at[v, row, 2], xr_sem.at[v, row, 2], (o, mate))

    for v in range(vecs):
        mated(v, mate, s, lambda c: c.start())

        @pl.loop(2, ns)
        def _(k):
            t = partner(k, 1)
            middle(v, s, t, k).start()
            outer(v, s, t, k, lambda c: c.start())

    loads[0].wait()
    for p in range(pairs):
        hi, lo = split(rv[p, 0].T)
        wr[p, :b, :b] = hi
        wr[p, :b, b:] = lo
        wr[p, b:, :b] = hi
        wr[p, b:, b:] = jnp.zeros((b, b), bf16)

    def contract_right(v, q):
        for p in range(pairs):
            d = rlinks[p, 0] - (s - 1)
            x = jnp.where(d == 0, wave[v, q, 0], jnp.where(d == 1, wave[v, q, 1], wave[v, q, 2]))
            hi, lo = split(x)
            y = dot(jnp.concatenate([hi, lo], axis=1), wr[p])
            hi, lo = split(y[:, :b] + y[:, b:])
            inner[v, p, q, :, :b] = hi
            inner[v, p, q, :, b:] = lo

    def contract_left(v, i):
        pieces = [split(lv[p, i]) for p in range(pairs)]
        picked = jnp.concatenate([inner[v, p, llinks[p, i]] for p in range(pairs)], axis=0)
        y = dot(jnp.concatenate([c[0] for c in pieces], axis=1), picked)
        z = dot(jnp.concatenate([c[1] for c in pieces], axis=1), picked[:, :b])
        return y[:, :b] + y[:, b:] + z

    def scatter(v, k):
        return pltpu.make_async_remote_copy(
            src_ref=part.at[v, k], dst_ref=got.at[v, k],
            send_sem=ss_sem.at[v, k], recv_sem=sr_sem.at[v, k],
            device_id=(layer(k), s), device_id_type=pl.DeviceIdType.MESH)

    for v in range(vecs):
        own(v, lambda c: c.wait())
        contract_right(v, s)
        mated(v, s, mate, lambda c: c.wait_recv())
        contract_right(v, mate)

        @pl.loop(2, ns)
        def _(k):
            q = partner(k, -1)
            middle(v, q, s, k).wait_recv()
            forward(v, q, 2 * odd).start()

        @pl.loop(2, ns)
        def _(k):
            q = partner(k, -1)
            outer(v, q, s, k, lambda c: c.wait_recv())
            forward(v, q, 2 - 2 * odd).wait_recv()
            contract_right(v, q)

        if v == 0:
            loads[1].wait()

        @pl.loop(1, no)
        def _(k):
            for r in range(rows):
                part[v, k, r] = contract_left(v, layer(k) * rows + r)
            scatter(v, k).start()

        for r in range(rows):
            part[v, 0, r] = contract_left(v, o * rows + r)

    for v in range(vecs):
        @pl.loop(1, no)
        def _(k):
            scatter(v, k).wait_recv()
        for r in range(rows):
            total = part[v, 0, r]
            for k in range(1, no):
                total = total + got[v, k, r]
            out[v, r, 0] = total

    for v in range(vecs):
        mated(v, mate, s, lambda c: c.wait_send())

        @pl.loop(2, ns)
        def _(k):
            t = partner(k, 1)
            middle(v, s, t, k).wait_send()
            outer(v, s, t, k, lambda c: c.wait_send())
            forward(v, t, 2 * odd).wait_send()

        @pl.loop(1, no)
        def _(k):
            scatter(v, k).wait_send()


def on_device(psi, left, right, llinks, rlinks):
    ns, no = lax.axis_size("sec"), lax.axis_size("ops")
    vecs, _, nq, b, _ = psi.shape
    pairs, rows = left.shape[0], nq // no
    shapes = [((vecs, nq, SPAN, b, b), f32), (left.shape, f32), (right.shape, f32),
              ((pairs, 2 * b, 2 * b), bf16), ((vecs, pairs, nq, b, 2 * b), bf16),
              ((vecs, no, rows, b, b), f32), ((vecs, no, rows, b, b), f32)]
    need = sum(jnp.dtype(t).itemsize * functools.reduce(lambda x, y: x * y, d) for d, t in shapes)
    any_, smem, vmem = (pl.BlockSpec(memory_space=m) for m in (pl.ANY, pltpu.SMEM, pltpu.VMEM))
    return pl.pallas_call(
        functools.partial(kernel, ns, no),
        out_shape=jax.ShapeDtypeStruct((vecs, rows, 1, b, b), f32),
        in_specs=[any_, any_, any_, smem, smem],
        out_specs=vmem,
        scratch_shapes=[pltpu.VMEM(d, t) for d, t in shapes] + [
            pltpu.SemaphoreType.DMA((2,)), pltpu.SemaphoreType.DMA((vecs,)),
            pltpu.SemaphoreType.DMA((vecs, ns, 3)), pltpu.SemaphoreType.DMA((vecs, ns, 3)),
            pltpu.SemaphoreType.DMA((vecs, no)), pltpu.SemaphoreType.DMA((vecs, no))],
        compiler_params=pltpu.CompilerParams(
            collective_id=0, has_side_effects=True, vmem_limit_bytes=60 << 20),
    )(psi, left, right, llinks, rlinks)


def solution(mesh):
    return jax.shard_map(
        on_device,
        mesh=mesh,
        in_specs=(
            P(None, "sec", None, None, None),
            P("ops", None, None, None),
            P("ops", "sec", None, None),
            P("ops", None),
            P("ops", "sec"),
        ),
        out_specs=P(None, "ops", "sec", None, None),
        check_vma=False,
    )
```

```python
import functools

import jax
import jax.numpy as jnp
from jax import lax
from jax.experimental import pallas as pl
from jax.experimental.pallas import tpu as pltpu
from jax.sharding import PartitionSpec as P

f32, bf16 = jnp.float32, jnp.bfloat16
SPAN = 3


NEAR = 8


def xor(a, b, n):
    bit, total = 1, 0
    while bit < n:
        total = total + bit * lax.rem(a // bit + b // bit, 2)
        bit *= 2
    return total


def split(x):
    hi = x.astype(bf16)
    return hi, (x - hi.astype(f32)).astype(bf16)


def dot(a, b):
    return lax.dot_general(a, b, (((1,), (0,)), ((), ())), preferred_element_type=f32)


def kernel(ns, no, psi, left, right, links, out,
           wave, lv, rv, wr, inner, part, got, lkv, lk,
           load_sem, own_sem, xs_sem, xr_sem, ss_sem, sr_sem, zs_sem, zr_sem, fs_sem, fr_sem):
    vecs, _, nq, b, _ = psi.shape
    pairs = left.shape[0]
    rows = nq // no
    o, s = lax.axis_index("ops"), lax.axis_index("sec")

    odd = lax.rem(s, 2)
    mate = s + 1 - 2 * odd

    half, hp = no // 2, pairs // 2
    parity = lax.rem(o, 2)
    other = o + 1 - 2 * parity

    def peer(k):
        return lax.rem(s + k, ns)

    def layer(k):
        return lax.rem(o + k, no)

    def kin(k):
        return lax.rem(o // 2 + k, half)

    loads = [pltpu.make_async_copy(right.at[:, 0], rv.at[pl.ds(0, pairs)], load_sem.at[0]),
             pltpu.make_async_copy(links, lk.at[0], load_sem.at[1])]
    loads += [pltpu.make_async_copy(left.at[:, pl.ds((parity + 2 * m) * rows, rows)], lv.at[pl.ds(0, pairs), m],
                                    load_sem.at[2 + m]) for m in range(half)]
    for c in loads:
        c.start()
    def window(t, go):
        for case, lo, hi in ((t == 0, 1, 3), (t == nq - 1, 0, 2), ((t > 0) & (t < nq - 1), 0, 3)):
            @pl.when(case)
            def _():
                go(pl.ds(t - 1 + lo, hi - lo), pl.ds(lo, hi - lo))

    def own(v, go):
        window(s, lambda src, dst: go(pltpu.make_async_copy(
            psi.at[v, 0, src], wave.at[v, s, dst], own_sem.at[v])))

    for v in range(vecs):
        own(v, lambda c: c.start())

    barrier = pltpu.get_barrier_semaphore()

    @pl.loop(1, ns)
    def _(k):
        pl.semaphore_signal(barrier, inc=1, device_id=(o, peer(k)), device_id_type=pl.DeviceIdType.MESH)

    @pl.loop(1, no)
    def _(k):
        pl.semaphore_signal(barrier, inc=1, device_id=(layer(k), s), device_id_type=pl.DeviceIdType.MESH)

    pl.semaphore_wait(barrier, ns - 1 + no - 1)

    def remote(src, dst, send, recv, to):
        return pltpu.make_async_remote_copy(
            src_ref=src, dst_ref=dst, send_sem=send, recv_sem=recv,
            device_id=to, device_id_type=pl.DeviceIdType.MESH)

    def partner(k):
        return xor(s, k, ns)

    near = min(NEAR, ns)

    def direct(row):
        return lax.rem(row + o, 2) == 0

    def middle(v, row, t, k):
        return remote(psi.at[v, 0, t], wave.at[v, row, 1], xs_sem.at[v, k, 0], xr_sem.at[v, k, 0], (o, t))

    def outer(v, row, t, k, go):
        even = lax.rem(t, 2) == 0
        @pl.when(even & (t > 0))
        def _():
            go(remote(psi.at[v, 0, t - 1], wave.at[v, row, 0], xs_sem.at[v, k, 1], xr_sem.at[v, k, 1], (o, t)))
        @pl.when(jnp.logical_not(even) & (t < nq - 1))
        def _():
            go(remote(psi.at[v, 0, t + 1], wave.at[v, row, 2], xs_sem.at[v, k, 1], xr_sem.at[v, k, 1], (o, t)))

    def mated(v, t, row, go):
        window(t, lambda src, dst: go(remote(
            psi.at[v, 0, src], wave.at[v, row, dst], xs_sem.at[v, 1, 0], xr_sem.at[v, 1, 0], (o, mate))))

    def forward(v, row, slot):
        return remote(wave.at[v, row, 1], wave.at[v, row, slot], xs_sem.at[v, row, 2], xr_sem.at[v, row, 2], (o, mate))

    def lift(v, row, go, middle_too=True):
        def one(slot, j):
            go(remote(wave.at[v, row, slot], wave.at[v, row, slot], xs_sem.at[v, row, j], xr_sem.at[v, row, j], (other, s)))
        if middle_too:
            one(1, 3)
        else:
            @pl.when((odd == 0) & (s > 0))
            def _():
                one(0, 4)
            @pl.when((odd == 1) & (s < nq - 1))
            def _():
                one(2, 4)

    mine = pl.ds(pairs + odd * hp, hp)
    across = [remote(right.at[:, 0], rv.at[pl.ds(pairs, pairs)], zs_sem.at[0], zr_sem.at[0], (other, s)),
              remote(links, lkv, zs_sem.at[1], zr_sem.at[1], (other, s))]
    across += [remote(left.at[pl.ds(odd * hp, hp), pl.ds((1 - parity + 2 * m) * rows, rows)], lv.at[mine, m],
                      zs_sem.at[2 + m], zr_sem.at[2 + m], (other, s)) for m in range(half)]
    for c in across:
        c.start()

    def hand(m, which):
        part_of = pl.ds(pairs + which * hp, hp)
        return remote(lv.at[part_of, m], lv.at[part_of, m], fs_sem.at[m], fr_sem.at[m], (o, mate))

    for v in range(vecs):
        @pl.when(direct(s))
        def _():
            @pl.loop(near, ns)
            def _(k):
                t = partner(k)
                middle(v, s, t, k).start()
                outer(v, s, t, k, lambda c: c.start())

        mated(v, mate, s, lambda c: c.start())

        @pl.loop(2, near)
        def _(k):
            t = partner(k)
            middle(v, s, t, k).start()
            outer(v, s, t, k, lambda c: c.start())

    loads[0].wait()
    loads[1].wait()
    across[1].wait_recv()
    arrived = pltpu.make_async_copy(lkv, lk.at[1], load_sem.at[1])
    arrived.start()
    arrived.wait()
    across[0].wait_recv()

    def link(p, i):
        return lk[p // pairs, p % pairs, i]

    for p in range(2 * pairs):
        hi, lo = split(rv[p].T)
        wr[p, :b, :b] = hi
        wr[p, :b, b:] = lo
        wr[p, b:, :b] = hi
        wr[p, b:, b:] = jnp.zeros((b, b), bf16)

    def contract_right(v, q):
        for p in range(2 * pairs):
            d = link(p, nq) - (s - 1)
            x = jnp.where(d == 0, wave[v, q, 0], jnp.where(d == 1, wave[v, q, 1], wave[v, q, 2]))
            hi, lo = split(x)
            y = dot(jnp.concatenate([hi, lo], axis=1), wr[p])
            hi, lo = split(y[:, :b] + y[:, b:])
            inner[p, q, :, :b] = hi
            inner[p, q, :, b:] = lo

    def contract_left(m, r):
        i = (parity + 2 * m) * rows + r
        pieces = [split(lv[p, m, r]) for p in range(2 * pairs)]
        picked = jnp.concatenate([inner[p, link(p, i)] for p in range(2 * pairs)], axis=0)
        y = dot(jnp.concatenate([c[0] for c in pieces], axis=1), picked)
        z = dot(jnp.concatenate([c[1] for c in pieces], axis=1), picked[:, :b])
        return y[:, :b] + y[:, b:] + z

    def scatter(v, k):
        return remote(part.at[v, k], got.at[v, k], ss_sem.at[v, k], sr_sem.at[v, k], (parity + 2 * kin(k), s))

    for v in range(vecs):
        own(v, lambda c: c.wait())
        contract_right(v, s)
        mated(v, s, mate, lambda c: c.wait_recv())
        contract_right(v, mate)

        @pl.loop(near, ns)
        def _(k):
            q = partner(k)

            @pl.when(direct(q))
            def _():
                middle(v, q, s, k).wait_recv()
                lift(v, q, lambda c: c.start())
                forward(v, q, 2 * odd).start()
                outer(v, q, s, k, lambda c: c.wait_recv())
                lift(v, q, lambda c: c.start(), False)

        @pl.loop(2, near)
        def _(k):
            q = partner(k)
            middle(v, q, s, k).wait_recv()
            forward(v, q, 2 * odd).start()

        @pl.loop(2, near)
        def _(k):
            q = partner(k)
            outer(v, q, s, k, lambda c: c.wait_recv())
            forward(v, q, 2 - 2 * odd).wait_recv()
            contract_right(v, q)

        @pl.loop(near, ns)
        def _(k):
            q = partner(k)

            @pl.when(jnp.logical_not(direct(q)))
            def _():
                lift(v, q, lambda c: c.wait_recv())
                forward(v, q, 2 * odd).start()
                lift(v, q, lambda c: c.wait_recv(), False)

        @pl.loop(near, ns)
        def _(k):
            q = partner(k)
            forward(v, q, 2 - 2 * odd).wait_recv()
            contract_right(v, q)

        if v == 0:
            for m in range(half):
                across[2 + m].wait_recv()
                hand(m, odd).start()
            for m in range(half):
                loads[2 + m].wait()
                hand(m, 1 - odd).wait_recv()

        @pl.loop(1, half)
        def _(k):
            for r in range(rows):
                part[v, k, r] = contract_left(kin(k), r)
            scatter(v, k).start()

        for r in range(rows):
            part[v, 0, r] = contract_left(kin(0), r)

    for v in range(vecs):
        @pl.loop(1, half)
        def _(k):
            scatter(v, k).wait_recv()
        for r in range(rows):
            total = part[v, 0, r]
            for k in range(1, half):
                total = total + got[v, k, r]
            out[v, r, 0] = total

    for c in across:
        c.wait_send()
    for m in range(half):
        hand(m, odd).wait_send()

    for v in range(vecs):
        mated(v, mate, s, lambda c: c.wait_send())

        @pl.loop(2, near)
        def _(k):
            t = partner(k)
            middle(v, s, t, k).wait_send()
            outer(v, s, t, k, lambda c: c.wait_send())
            forward(v, t, 2 * odd).wait_send()

        @pl.loop(near, ns)
        def _(k):
            t = partner(k)
            forward(v, t, 2 * odd).wait_send()

            @pl.when(direct(s))
            def _():
                middle(v, s, t, k).wait_send()
                outer(v, s, t, k, lambda c: c.wait_send())

            @pl.when(direct(t))
            def _():
                lift(v, t, lambda c: c.wait_send())
                lift(v, t, lambda c: c.wait_send(), False)

        @pl.loop(1, half)
        def _(k):
            scatter(v, k).wait_send()


def on_device(psi, left, right, llinks, rlinks):
    ns, no = lax.axis_size("sec"), lax.axis_size("ops")
    vecs, _, nq, b, _ = psi.shape
    pairs, rows, half = left.shape[0], nq // no, no // 2
    links = jnp.concatenate([llinks, rlinks], axis=1)
    links = jnp.pad(links, ((0, -pairs % 8), (0, -(nq + 1) % 128)))
    shapes = [((vecs, nq, SPAN, b, b), f32), ((2 * pairs, half, rows, b, b), f32), ((2 * pairs, b, b), f32),
              ((2 * pairs, 2 * b, 2 * b), bf16), ((2 * pairs, nq, b, 2 * b), bf16),
              ((vecs, half, rows, b, b), f32), ((vecs, half, rows, b, b), f32), (links.shape, jnp.int32)]
    any_, vmem = (pl.BlockSpec(memory_space=m) for m in (pl.ANY, pltpu.VMEM))
    dma = pltpu.SemaphoreType.DMA
    return pl.pallas_call(
        functools.partial(kernel, ns, no),
        out_shape=jax.ShapeDtypeStruct((vecs, rows, 1, b, b), f32),
        in_specs=[any_] * 4,
        out_specs=vmem,
        scratch_shapes=[pltpu.VMEM(d, t) for d, t in shapes] + [
            pltpu.SMEM((2, *links.shape), jnp.int32), dma((2 + half,)), dma((vecs,)),
            dma((vecs, ns, 5)), dma((vecs, ns, 5)), dma((vecs, half)), dma((vecs, half)),
            dma((2 + half,)), dma((2 + half,)), dma((half,)), dma((half,))],
        compiler_params=pltpu.CompilerParams(
            collective_id=0, has_side_effects=True, vmem_limit_bytes=60 << 20),
    )(psi, left, right, links)


def solution(mesh):
    return jax.shard_map(
        on_device,
        mesh=mesh,
        in_specs=(
            P(None, "sec", None, None, None),
            P("ops", None, None, None),
            P("ops", "sec", None, None),
            P("ops", None),
            P("ops", "sec"),
        ),
        out_specs=P(None, "ops", "sec", None, None),
        check_vma=False,
    )
```

```python
import functools

import jax
import jax.numpy as jnp
from jax import lax
from jax.experimental import pallas as pl
from jax.experimental.pallas import tpu as pltpu
from jax.sharding import PartitionSpec as P

f32, bf16 = jnp.float32, jnp.bfloat16
SPAN = 3


NEAR = 8


def xor(a, b, n):
    bit, total = 1, 0
    while bit < n:
        total = total + bit * lax.rem(a // bit + b // bit, 2)
        bit *= 2
    return total


def split(x):
    hi = x.astype(bf16)
    return hi, (x - hi.astype(f32)).astype(bf16)


def dot(a, b):
    return lax.dot_general(a, b, (((1,), (0,)), ((), ())), preferred_element_type=f32)


def kernel(ns, no, psi, left, right, llinks, rlinks, out,
           wave, lv, rv, wr, inner, part, got, links, lkv, lk,
           load_sem, own_sem, xs_sem, xr_sem, ss_sem, sr_sem, zs_sem, zr_sem, fs_sem, fr_sem):
    vecs, _, nq, b, _ = psi.shape
    pairs = left.shape[0]
    rows = nq // no
    o, s = lax.axis_index("ops"), lax.axis_index("sec")

    odd = lax.rem(s, 2)
    mate = s + 1 - 2 * odd

    half, hp = no // 2, pairs // 2
    parity = lax.rem(o, 2)
    other = o + 1 - 2 * parity

    def peer(k):
        return lax.rem(s + k, ns)

    def layer(k):
        return lax.rem(o + k, no)

    def kin(k):
        return lax.rem(o // 2 + k, half)

    links[...] = jnp.zeros_like(links)
    links[:pairs, :nq] = llinks[...]
    links[pairs:pairs + 1, :pairs] = rlinks[...]
    loads = [pltpu.make_async_copy(right.at[:, 0], rv.at[pl.ds(0, pairs)], load_sem.at[0]),
             pltpu.make_async_copy(links, lk.at[0], load_sem.at[1])]
    loads += [pltpu.make_async_copy(left.at[:, pl.ds((parity + 2 * m) * rows, rows)], lv.at[pl.ds(0, pairs), m],
                                    load_sem.at[2 + m]) for m in range(half)]
    for c in loads:
        c.start()
    def window(t, go):
        for case, lo, hi in ((t == 0, 1, 3), (t == nq - 1, 0, 2), ((t > 0) & (t < nq - 1), 0, 3)):
            @pl.when(case)
            def _():
                go(pl.ds(t - 1 + lo, hi - lo), pl.ds(lo, hi - lo))

    def own(v, go):
        window(s, lambda src, dst: go(pltpu.make_async_copy(
            psi.at[v, 0, src], wave.at[v, s, dst], own_sem.at[v])))

    for v in range(vecs):
        own(v, lambda c: c.start())

    barrier = pltpu.get_barrier_semaphore()

    @pl.loop(1, ns)
    def _(k):
        pl.semaphore_signal(barrier, inc=1, device_id=(o, peer(k)), device_id_type=pl.DeviceIdType.MESH)

    @pl.loop(1, no)
    def _(k):
        pl.semaphore_signal(barrier, inc=1, device_id=(layer(k), s), device_id_type=pl.DeviceIdType.MESH)

    pl.semaphore_wait(barrier, ns - 1 + no - 1)

    def remote(src, dst, send, recv, to):
        return pltpu.make_async_remote_copy(
            src_ref=src, dst_ref=dst, send_sem=send, recv_sem=recv,
            device_id=to, device_id_type=pl.DeviceIdType.MESH)

    def partner(k):
        return xor(s, k, ns)

    near = min(NEAR, ns)

    def direct(row):
        return lax.rem(row + o, 2) == 0

    def middle(v, row, t, k):
        return remote(psi.at[v, 0, t], wave.at[v, row, 1], xs_sem.at[v, k, 0], xr_sem.at[v, k, 0], (o, t))

    def outer(v, row, t, k, go):
        even = lax.rem(t, 2) == 0
        @pl.when(even & (t > 0))
        def _():
            go(remote(psi.at[v, 0, t - 1], wave.at[v, row, 0], xs_sem.at[v, k, 1], xr_sem.at[v, k, 1], (o, t)))
        @pl.when(jnp.logical_not(even) & (t < nq - 1))
        def _():
            go(remote(psi.at[v, 0, t + 1], wave.at[v, row, 2], xs_sem.at[v, k, 1], xr_sem.at[v, k, 1], (o, t)))

    def mated(v, t, row, go):
        window(t, lambda src, dst: go(remote(
            psi.at[v, 0, src], wave.at[v, row, dst], xs_sem.at[v, 1, 0], xr_sem.at[v, 1, 0], (o, mate))))

    def forward(v, row, slot):
        return remote(wave.at[v, row, 1], wave.at[v, row, slot], xs_sem.at[v, row, 2], xr_sem.at[v, row, 2], (o, mate))

    def lift(v, row, go, middle_too=True):
        def one(slot, j):
            go(remote(wave.at[v, row, slot], wave.at[v, row, slot], xs_sem.at[v, row, j], xr_sem.at[v, row, j], (other, s)))
        if middle_too:
            one(1, 3)
        else:
            @pl.when((odd == 0) & (s > 0))
            def _():
                one(0, 4)
            @pl.when((odd == 1) & (s < nq - 1))
            def _():
                one(2, 4)

    turns = [*range(1, half), 0]
    mine = pl.ds(pairs + odd * hp, hp)
    across = [remote(right.at[:, 0], rv.at[pl.ds(pairs, pairs)], zs_sem.at[0], zr_sem.at[0], (other, s)),
              remote(links, lkv, zs_sem.at[half + 1], zr_sem.at[half + 1], (other, s))]
    across += [remote(left.at[pl.ds(odd * hp, hp), pl.ds((1 - parity + 2 * kin(m)) * rows, rows)], lv.at[mine, kin(m)],
                      zs_sem.at[1 + m], zr_sem.at[1 + m], (other, s)) for m in turns]
    for c in across:
        c.start()

    def hand(m, which):
        part_of = pl.ds(pairs + which * hp, hp)
        return remote(lv.at[part_of, kin(m)], lv.at[part_of, kin(m)], fs_sem.at[m], fr_sem.at[m], (o, mate))

    for v in range(vecs):
        @pl.when(direct(s))
        def _():
            @pl.loop(near, ns)
            def _(k):
                t = partner(k)
                middle(v, s, t, k).start()
                outer(v, s, t, k, lambda c: c.start())

        mated(v, mate, s, lambda c: c.start())

        @pl.loop(2, near)
        def _(k):
            t = partner(k)
            middle(v, s, t, k).start()
            outer(v, s, t, k, lambda c: c.start())

    loads[0].wait()
    loads[1].wait()
    across[1].wait_recv()
    arrived = pltpu.make_async_copy(lkv, lk.at[1], load_sem.at[1])
    arrived.start()
    arrived.wait()
    across[0].wait_recv()

    def left_link(p, i):
        return lk[p // pairs, p % pairs, i]

    def right_link(p):
        return lk[p // pairs, pairs, p % pairs]

    for p in range(2 * pairs):
        hi, lo = split(rv[p].T)
        wr[p, :b, :b] = hi
        wr[p, :b, b:] = lo
        wr[p, b:, :b] = hi
        wr[p, b:, b:] = jnp.zeros((b, b), bf16)

    def contract_right(v, q):
        for p in range(2 * pairs):
            d = right_link(p) - (s - 1)
            x = jnp.where(d == 0, wave[v, q, 0], jnp.where(d == 1, wave[v, q, 1], wave[v, q, 2]))
            hi, lo = split(x)
            y = dot(jnp.concatenate([hi, lo], axis=1), wr[p])
            hi, lo = split(y[:, :b] + y[:, b:])
            inner[p, q, :, :b] = hi
            inner[p, q, :, b:] = lo

    def contract_left(m, r):
        i = (parity + 2 * m) * rows + r
        pieces = [split(lv[p, m, r]) for p in range(2 * pairs)]
        picked = jnp.concatenate([inner[p, left_link(p, i)] for p in range(2 * pairs)], axis=0)
        y = dot(jnp.concatenate([c[0] for c in pieces], axis=1), picked)
        z = dot(jnp.concatenate([c[1] for c in pieces], axis=1), picked[:, :b])
        return y[:, :b] + y[:, b:] + z

    def scatter(v, k):
        return remote(part.at[v, k], got.at[v, k], ss_sem.at[v, k], sr_sem.at[v, k], (parity + 2 * kin(k), s))

    for v in range(vecs):
        own(v, lambda c: c.wait())
        contract_right(v, s)
        mated(v, s, mate, lambda c: c.wait_recv())
        contract_right(v, mate)

        @pl.loop(near, ns)
        def _(k):
            q = partner(k)

            @pl.when(direct(q))
            def _():
                middle(v, q, s, k).wait_recv()
                lift(v, q, lambda c: c.start())
                forward(v, q, 2 * odd).start()
                outer(v, q, s, k, lambda c: c.wait_recv())
                lift(v, q, lambda c: c.start(), False)

        @pl.loop(2, near)
        def _(k):
            q = partner(k)
            middle(v, q, s, k).wait_recv()
            forward(v, q, 2 * odd).start()

        @pl.loop(2, near)
        def _(k):
            q = partner(k)
            outer(v, q, s, k, lambda c: c.wait_recv())
            forward(v, q, 2 - 2 * odd).wait_recv()
            contract_right(v, q)

        @pl.loop(near, ns)
        def _(k):
            q = partner(k)

            @pl.when(jnp.logical_not(direct(q)))
            def _():
                lift(v, q, lambda c: c.wait_recv())
                forward(v, q, 2 * odd).start()
                lift(v, q, lambda c: c.wait_recv(), False)

        @pl.loop(near, ns)
        def _(k):
            q = partner(k)
            forward(v, q, 2 - 2 * odd).wait_recv()
            contract_right(v, q)

        for place, k in enumerate(turns):
            if v == 0:
                across[2 + place].wait_recv()
                hand(k, odd).start()
                if place == 0:
                    for m in range(half):
                        loads[2 + m].wait()
                hand(k, 1 - odd).wait_recv()
            for r in range(rows):
                part[v, k, r] = contract_left(kin(k), r)
            if k > 0:
                scatter(v, k).start()

    for v in range(vecs):
        @pl.loop(1, half)
        def _(k):
            scatter(v, k).wait_recv()
        for r in range(rows):
            total = part[v, 0, r]
            for k in range(1, half):
                total = total + got[v, k, r]
            out[v, r, 0] = total

    for c in across:
        c.wait_send()
    for m in range(half):
        hand(m, odd).wait_send()

    for v in range(vecs):
        mated(v, mate, s, lambda c: c.wait_send())

        @pl.loop(2, near)
        def _(k):
            t = partner(k)
            middle(v, s, t, k).wait_send()
            outer(v, s, t, k, lambda c: c.wait_send())
            forward(v, t, 2 * odd).wait_send()

        @pl.loop(near, ns)
        def _(k):
            t = partner(k)
            forward(v, t, 2 * odd).wait_send()

            @pl.when(direct(s))
            def _():
                middle(v, s, t, k).wait_send()
                outer(v, s, t, k, lambda c: c.wait_send())

            @pl.when(direct(t))
            def _():
                lift(v, t, lambda c: c.wait_send())
                lift(v, t, lambda c: c.wait_send(), False)

        @pl.loop(1, half)
        def _(k):
            scatter(v, k).wait_send()


def on_device(psi, left, right, llinks, rlinks):
    ns, no = lax.axis_size("sec"), lax.axis_size("ops")
    vecs, _, nq, b, _ = psi.shape
    pairs, rows, half = left.shape[0], nq // no, no // 2
    table = (pairs + 8 - pairs % 8, nq + -nq % 128)
    shapes = [((vecs, nq, SPAN, b, b), f32), ((2 * pairs, half, rows, b, b), f32), ((2 * pairs, b, b), f32),
              ((2 * pairs, 2 * b, 2 * b), bf16), ((2 * pairs, nq, b, 2 * b), bf16),
              ((vecs, half, rows, b, b), f32), ((vecs, half, rows, b, b), f32), (table, jnp.int32), (table, jnp.int32)]
    any_, vmem = (pl.BlockSpec(memory_space=m) for m in (pl.ANY, pltpu.VMEM))
    dma = pltpu.SemaphoreType.DMA
    return pl.pallas_call(
        functools.partial(kernel, ns, no),
        out_shape=jax.ShapeDtypeStruct((vecs, rows, 1, b, b), f32),
        in_specs=[any_] * 3 + [vmem] * 2,
        out_specs=vmem,
        scratch_shapes=[pltpu.VMEM(d, t) for d, t in shapes] + [
            pltpu.SMEM((2, *table), jnp.int32), dma((2 + half,)), dma((vecs,)),
            dma((vecs, ns, 5)), dma((vecs, ns, 5)), dma((vecs, half)), dma((vecs, half)),
            dma((2 + half,)), dma((2 + half,)), dma((half,)), dma((half,))],
        compiler_params=pltpu.CompilerParams(
            collective_id=0, has_side_effects=True, vmem_limit_bytes=60 << 20),
    )(psi, left, right, llinks, rlinks.T)


def solution(mesh):
    return jax.shard_map(
        on_device,
        mesh=mesh,
        in_specs=(
            P(None, "sec", None, None, None),
            P("ops", None, None, None),
            P("ops", "sec", None, None),
            P("ops", None),
            P("ops", "sec"),
        ),
        out_specs=P(None, "ops", "sec", None, None),
        check_vma=False,
    )
```

```python
import functools

import jax
import jax.numpy as jnp
from jax import lax
from jax.experimental import pallas as pl
from jax.experimental.pallas import tpu as pltpu
from jax.sharding import PartitionSpec as P

f32, bf16 = jnp.float32, jnp.bfloat16
SPAN = 3


NEAR = 8


def xor(a, b, n):
    bit, total = 1, 0
    while bit < n:
        total = total + bit * lax.rem(a // bit + b // bit, 2)
        bit *= 2
    return total


def split(x):
    hi = x.astype(bf16)
    return hi, (x - hi.astype(f32)).astype(bf16)


def dot(a, b):
    return lax.dot_general(a, b, (((1,), (0,)), ((), ())), preferred_element_type=f32)


def kernel(ns, no, psi, left, right, llinks, rlinks, out,
           wave, lv, rv, wr, inner, part, got, links, lkv, lk,
           load_sem, own_sem, xs_sem, xr_sem, ss_sem, sr_sem, zs_sem, zr_sem, fs_sem, fr_sem):
    vecs, _, nq, b, _ = psi.shape
    pairs = left.shape[0]
    rows = nq // no
    o, s = lax.axis_index("ops"), lax.axis_index("sec")

    odd = lax.rem(s, 2)
    mate = s + 1 - 2 * odd

    half, hp = no // 2, pairs // 2
    parity = lax.rem(o, 2)
    other = o + 1 - 2 * parity

    def peer(k):
        return lax.rem(s + k, ns)

    def layer(k):
        return lax.rem(o + k, no)

    def kin(k):
        return lax.rem(o // 2 + k, half)

    links[...] = jnp.zeros_like(links)
    links[:pairs, :nq] = llinks[...]
    links[pairs:pairs + 1, :pairs] = rlinks[...]
    loads = [pltpu.make_async_copy(right.at[:, 0], rv.at[pl.ds(0, pairs)], load_sem.at[0]),
             pltpu.make_async_copy(links, lk.at[0], load_sem.at[1])]
    loads += [pltpu.make_async_copy(left.at[:, pl.ds((parity + 2 * m) * rows, rows)], lv.at[pl.ds(0, pairs), m],
                                    load_sem.at[2 + m]) for m in range(half)]
    for c in loads:
        c.start()
    def window(t, go):
        for case, lo, hi in ((t == 0, 1, 3), (t == nq - 1, 0, 2), ((t > 0) & (t < nq - 1), 0, 3)):
            @pl.when(case)
            def _():
                go(pl.ds(t - 1 + lo, hi - lo), pl.ds(lo, hi - lo))

    def own(v, go):
        window(s, lambda src, dst: go(pltpu.make_async_copy(
            psi.at[v, 0, src], wave.at[v, s, dst], own_sem.at[v])))

    for v in range(vecs):
        own(v, lambda c: c.start())

    barrier = pltpu.get_barrier_semaphore()

    @pl.loop(1, ns)
    def _(k):
        pl.semaphore_signal(barrier, inc=1, device_id=(o, peer(k)), device_id_type=pl.DeviceIdType.MESH)

    @pl.loop(1, no)
    def _(k):
        pl.semaphore_signal(barrier, inc=1, device_id=(layer(k), s), device_id_type=pl.DeviceIdType.MESH)

    pl.semaphore_wait(barrier, ns - 1 + no - 1)

    def remote(src, dst, send, recv, to):
        return pltpu.make_async_remote_copy(
            src_ref=src, dst_ref=dst, send_sem=send, recv_sem=recv,
            device_id=to, device_id_type=pl.DeviceIdType.MESH)

    def partner(k):
        return xor(s, k, ns)

    near = min(NEAR, ns)

    def direct(row):
        return lax.rem(row + o, 2) == 0

    def middle(v, row, t, k):
        return remote(psi.at[v, 0, t], wave.at[v, row, 1], xs_sem.at[v, k, 0], xr_sem.at[v, k, 0], (o, t))

    def outer(v, row, t, k, go):
        even = lax.rem(t, 2) == 0
        @pl.when(even & (t > 0))
        def _():
            go(remote(psi.at[v, 0, t - 1], wave.at[v, row, 0], xs_sem.at[v, k, 1], xr_sem.at[v, k, 1], (o, t)))
        @pl.when(jnp.logical_not(even) & (t < nq - 1))
        def _():
            go(remote(psi.at[v, 0, t + 1], wave.at[v, row, 2], xs_sem.at[v, k, 1], xr_sem.at[v, k, 1], (o, t)))

    def mated(v, t, row, go):
        window(t, lambda src, dst: go(remote(
            psi.at[v, 0, src], wave.at[v, row, dst], xs_sem.at[v, 1, 0], xr_sem.at[v, 1, 0], (o, mate))))

    def forward(v, row, slot):
        return remote(wave.at[v, row, 1], wave.at[v, row, slot], xs_sem.at[v, row, 2], xr_sem.at[v, row, 2], (o, mate))

    def lift(v, row, go, middle_too=True):
        def one(slot, j):
            go(remote(wave.at[v, row, slot], wave.at[v, row, slot], xs_sem.at[v, row, j], xr_sem.at[v, row, j], (other, s)))
        if middle_too:
            one(1, 3)
        else:
            @pl.when((odd == 0) & (s > 0))
            def _():
                one(0, 4)
            @pl.when((odd == 1) & (s < nq - 1))
            def _():
                one(2, 4)

    turns = [*range(1, half), 0]
    mine = pl.ds(pairs + odd * hp, hp)
    across = [remote(right.at[:, 0], rv.at[pl.ds(pairs, pairs)], zs_sem.at[0], zr_sem.at[0], (other, s)),
              remote(links, lkv, zs_sem.at[half + 1], zr_sem.at[half + 1], (other, s))]
    across += [remote(left.at[pl.ds(odd * hp, hp), pl.ds((1 - parity + 2 * kin(m)) * rows, rows)], lv.at[mine, kin(m)],
                      zs_sem.at[1 + m], zr_sem.at[1 + m], (other, s)) for m in turns]
    for c in across:
        c.start()

    def hand(m, which):
        part_of = pl.ds(pairs + which * hp, hp)
        return remote(lv.at[part_of, kin(m)], lv.at[part_of, kin(m)], fs_sem.at[m], fr_sem.at[m], (o, mate))

    for v in range(vecs):
        @pl.when(direct(s))
        def _():
            @pl.loop(near, ns)
            def _(k):
                t = partner(k)
                middle(v, s, t, k).start()
                outer(v, s, t, k, lambda c: c.start())

        mated(v, mate, s, lambda c: c.start())

        @pl.loop(2, near)
        def _(k):
            t = partner(k)
            middle(v, s, t, k).start()
            outer(v, s, t, k, lambda c: c.start())

    loads[0].wait()
    loads[1].wait()
    across[1].wait_recv()
    arrived = pltpu.make_async_copy(lkv, lk.at[1], load_sem.at[1])
    arrived.start()
    arrived.wait()
    across[0].wait_recv()

    def left_link(p, i):
        return lk[p // pairs, p % pairs, i]

    def right_link(p):
        return lk[p // pairs, pairs, p % pairs]

    for p in range(2 * pairs):
        hi, lo = split(rv[p].T)
        wr[p, :b, :b] = hi
        wr[p, :b, b:] = lo
        wr[p, b:, :b] = hi
        wr[p, b:, b:] = jnp.zeros((b, b), bf16)

    def contract_right(v, q):
        for p in range(2 * pairs):
            d = right_link(p) - (s - 1)
            x = jnp.where(d == 0, wave[v, q, 0], jnp.where(d == 1, wave[v, q, 1], wave[v, q, 2]))
            hi, lo = split(x)
            y = dot(jnp.concatenate([hi, lo], axis=1), wr[p])
            hi, lo = split(y[:, :b] + y[:, b:])
            inner[p, q, :, :b] = hi
            inner[p, q, :, b:] = lo

    def contract_left(m, r):
        i = (parity + 2 * m) * rows + r
        pieces = [split(lv[p, m, r]) for p in range(2 * pairs)]
        picked = jnp.concatenate([inner[p, left_link(p, i)] for p in range(2 * pairs)], axis=0)
        y = dot(jnp.concatenate([c[0] for c in pieces], axis=1), picked)
        z = dot(jnp.concatenate([c[1] for c in pieces], axis=1), picked[:, :b])
        return y[:, :b] + y[:, b:] + z

    def scatter(v, k, r):
        return remote(part.at[v, k, r], got.at[v, k, r], ss_sem.at[v, k, r], sr_sem.at[v, k, r], (parity + 2 * kin(k), s))

    for v in range(vecs):
        own(v, lambda c: c.wait())
        contract_right(v, s)
        mated(v, s, mate, lambda c: c.wait_recv())
        contract_right(v, mate)

        @pl.loop(near, ns)
        def _(k):
            q = partner(k)

            @pl.when(direct(q))
            def _():
                middle(v, q, s, k).wait_recv()
                lift(v, q, lambda c: c.start())
                forward(v, q, 2 * odd).start()
                outer(v, q, s, k, lambda c: c.wait_recv())
                lift(v, q, lambda c: c.start(), False)

        @pl.loop(2, near)
        def _(k):
            q = partner(k)
            middle(v, q, s, k).wait_recv()
            forward(v, q, 2 * odd).start()

        @pl.loop(2, near)
        def _(k):
            q = partner(k)
            outer(v, q, s, k, lambda c: c.wait_recv())
            forward(v, q, 2 - 2 * odd).wait_recv()
            contract_right(v, q)

        @pl.loop(near, ns)
        def _(k):
            q = partner(k)

            @pl.when(jnp.logical_not(direct(q)))
            def _():
                lift(v, q, lambda c: c.wait_recv())
                forward(v, q, 2 * odd).start()
                lift(v, q, lambda c: c.wait_recv(), False)

        @pl.loop(near, ns)
        def _(k):
            q = partner(k)
            forward(v, q, 2 - 2 * odd).wait_recv()
            contract_right(v, q)

        for place, k in enumerate(turns):
            if v == 0:
                across[2 + place].wait_recv()
                hand(k, odd).start()
                if place == 0:
                    for m in range(half):
                        loads[2 + m].wait()
                hand(k, 1 - odd).wait_recv()
            for r in range(rows):
                part[v, k, r] = contract_left(kin(k), r)
                if k > 0:
                    scatter(v, k, r).start()

    for v in range(vecs):
        for r in range(rows):
            for k in range(1, half):
                scatter(v, k, r).wait_recv()
            total = part[v, 0, r]
            for k in range(1, half):
                total = total + got[v, k, r]
            out[v, r, 0] = total

    for c in across:
        c.wait_send()
    for m in range(half):
        hand(m, odd).wait_send()

    for v in range(vecs):
        mated(v, mate, s, lambda c: c.wait_send())

        @pl.loop(2, near)
        def _(k):
            t = partner(k)
            middle(v, s, t, k).wait_send()
            outer(v, s, t, k, lambda c: c.wait_send())
            forward(v, t, 2 * odd).wait_send()

        @pl.loop(near, ns)
        def _(k):
            t = partner(k)
            forward(v, t, 2 * odd).wait_send()

            @pl.when(direct(s))
            def _():
                middle(v, s, t, k).wait_send()
                outer(v, s, t, k, lambda c: c.wait_send())

            @pl.when(direct(t))
            def _():
                lift(v, t, lambda c: c.wait_send())
                lift(v, t, lambda c: c.wait_send(), False)

        @pl.loop(1, half)
        def _(k):
            for r in range(rows):
                scatter(v, k, r).wait_send()


def on_device(psi, left, right, llinks, rlinks):
    ns, no = lax.axis_size("sec"), lax.axis_size("ops")
    vecs, _, nq, b, _ = psi.shape
    pairs, rows, half = left.shape[0], nq // no, no // 2
    table = (pairs + 8 - pairs % 8, nq + -nq % 128)
    shapes = [((vecs, nq, SPAN, b, b), f32), ((2 * pairs, half, rows, b, b), f32), ((2 * pairs, b, b), f32),
              ((2 * pairs, 2 * b, 2 * b), bf16), ((2 * pairs, nq, b, 2 * b), bf16),
              ((vecs, half, rows, b, b), f32), ((vecs, half, rows, b, b), f32), (table, jnp.int32), (table, jnp.int32)]
    any_, vmem = (pl.BlockSpec(memory_space=m) for m in (pl.ANY, pltpu.VMEM))
    dma = pltpu.SemaphoreType.DMA
    return pl.pallas_call(
        functools.partial(kernel, ns, no),
        out_shape=jax.ShapeDtypeStruct((vecs, rows, 1, b, b), f32),
        in_specs=[any_] * 3 + [vmem] * 2,
        out_specs=vmem,
        scratch_shapes=[pltpu.VMEM(d, t) for d, t in shapes] + [
            pltpu.SMEM((2, *table), jnp.int32), dma((2 + half,)), dma((vecs,)),
            dma((vecs, ns, 5)), dma((vecs, ns, 5)), dma((vecs, half, rows)), dma((vecs, half, rows)),
            dma((2 + half,)), dma((2 + half,)), dma((half,)), dma((half,))],
        compiler_params=pltpu.CompilerParams(
            collective_id=0, has_side_effects=True, vmem_limit_bytes=60 << 20),
    )(psi, left, right, llinks, rlinks.T)


def solution(mesh):
    return jax.shard_map(
        on_device,
        mesh=mesh,
        in_specs=(
            P(None, "sec", None, None, None),
            P("ops", None, None, None),
            P("ops", "sec", None, None),
            P("ops", None),
            P("ops", "sec"),
        ),
        out_specs=P(None, "ops", "sec", None, None),
        check_vma=False,
    )
```
